32 devices in a mesh: comp: 8 (over y, x, core), space: 4 (over z).
Axes of the slice: x: 2, y: 2, z: 4, core: 2. Of those that a mesh axis runs over, the one named last changes fastest.
Arguments:
- concentration: float32 [16, 16, 64, 2048], P('comp', None, 'space'), may hold values from -3 to 3
- phase_labels: int32 [16, 64, 2048], P(None, 'space'), may hold values from 0 to 3
- hessian: float32 [4, 16, 16], replicated, may hold values from -1.5 to 1.5
- mobility: float32 [4, 16], replicated, may hold values from 0.2 to 2
Outputs:
- new_concentration: float32 [16, 16, 64, 2048], P('comp', None, 'space')
- potential: float32 [16, 16, 64, 2048], P('comp', None, 'space')
The draws below stay inside these ranges and needn't reach their ends.
All inputs are finite; a program needn't handle non-finite values.
Results may differ from the reference program's by a relative error of at most 0.00017.
Values sent between devices are 32-bit elements; how exact they have to be, the bound alone decides.
A program may use at most 192 MiB of HBM per device.

```python
import math
import jax
import jax.numpy as jnp
from jax import lax

C = 16
PHASES = 4
SWEEPS = 2
NY = 2048
NZ = 16
NX = 64


def with_ends(result, own_key, low, high):
    longest = result.shape.index(max(result.shape))
    spots = []
    for shift in (0, 1):
        where = [jax.random.randint(jax.random.fold_in(own_key, axis), (), 0, length) for axis, length in enumerate(result.shape)]
        where[longest] = (where[longest] + shift) % result.shape[longest]
        spots.append(tuple(where))
    return result.at[spots[0]].set(low).at[spots[1]].set(high)


def block_levels(rng, extent, pieces, smallest, top_value):
    level, own = 1.0, jax.random.fold_in(rng, 6)
    for dim, blocks in pieces:
        heights = jnp.exp(jax.random.uniform(jax.random.fold_in(own, dim), (blocks,), jnp.float32, smallest / len(pieces), top_value / len(pieces)))
        level = level * jnp.repeat(heights, extent[dim] // blocks).reshape([-1 if axis == dim else 1 for axis in range(len(extent))])
    return level


def normal_values(rng, shape, width, limit, shards=(), held_as=jnp.bfloat16):
    loudness = block_levels(rng, shape, shards, -0.22, 0.18) if shards else 1.0
    result = jax.random.normal(rng, shape, jnp.float32) * width * loudness
    return jnp.minimum(jnp.maximum(result, -limit), limit).astype(held_as)


def setup_inputs(seed: int = 0) -> dict:
    key_list = jax.random.split(jax.random.key(seed), 5)
    concentration = normal_values(key_list[0], (C, NZ, NX, NY), 0.5, 3.0, ((0, 8), (2, 4)), jnp.float32)
    phase_labels = with_ends(jax.random.randint(key_list[1], (NZ, NX, NY), 0, PHASES), jax.random.fold_in(key_list[1], 1), 0, PHASES - 1).astype(jnp.int32)
    hessian = normal_values(key_list[2], (PHASES, C, C), 0.25, 1.5, (), jnp.float32)
    mobility = jnp.clip(jnp.exp(jax.random.uniform(key_list[3], (PHASES, C), jnp.float32, math.log(0.2), math.log(2.0))), 0.2, 2.0)
    return dict(concentration=concentration, phase_labels=phase_labels, hessian=hessian, mobility=mobility)


time_step = 0.1
stiff_step = 0.02
damping = 0.5


def laplace(field):
    summed = jnp.roll(field, 1, 2) + jnp.roll(field, -1, 2)
    summed = summed + jnp.roll(field, 1, 3) + jnp.roll(field, -1, 3)
    summed = summed + jnp.roll(field, 1, 1) + jnp.roll(field, -1, 1)
    return summed - 6.0 * field


def reference(concentration, phase_labels, hessian, mobility):
    coupled = jnp.zeros(concentration.shape, jnp.float32)
    for phase in range(PHASES):
        product = jnp.einsum("ij,jzxy->izxy", hessian[phase], concentration, precision=lax.Precision.HIGHEST)
        coupled = coupled + jnp.where(phase_labels == phase, product, 0.0)
    potential = coupled + concentration * concentration * concentration
    mobile = mobility.T[:, phase_labels]
    source = concentration + time_step * mobile * laplace(potential)
    bilap_coef = stiff_step * mobile
    diagonal_term = 1.0 + 42.0 * bilap_coef
    iterate = source
    for sweep in range(SWEEPS):
        iterate = iterate + damping * (source - iterate - bilap_coef * laplace(laplace(iterate))) / diagonal_term
    return iterate, potential
```

```python
import functools

import jax
import jax.numpy as jnp
from jax import lax
from jax.experimental import pallas as pl
from jax.experimental.pallas import tpu as pltpu
from jax.sharding import PartitionSpec as P

SWEEPS = 2


time_step = 0.1
stiff_step = 0.02
damping = 0.5

MESH = pl.DeviceIdType.MESH
DEPTH = 3
LAG = 3
LANES = 256


def extended(shard, sides, width):
    for axis, dim in sides:
        devices, length = (lax.axis_size(axis), shard.shape[dim])
        up = [(i, (i + 1) % devices) for i in range(devices)]
        down = [(j, i) for i, j in up]
        last = lax.slice_in_dim(shard, length - width, length, axis=dim)
        initial = lax.slice_in_dim(shard, 0, width, axis=dim)
        before = lax.ppermute(last, axis, up)
        after = lax.ppermute(initial, axis, down)
        shard = jnp.concatenate([before, shard, after], axis=dim)
    return shard


def laplace_inner(field):
    centre = field[:, :, 1:-1, :]
    summed = field[:, :, 2:, :] + field[:, :, :-2, :]
    summed = summed + jnp.roll(centre, 1, 3) + jnp.roll(centre, -1, 3)
    summed = summed + jnp.roll(centre, 1, 1) + jnp.roll(centre, -1, 1)
    return summed - 6.0 * centre


def potential_kernel(
    inner, c_hbm, ph_hbm, h_ref, pot_hbm,
    gathered, labels, part_out, part_in, pot,
    xs, xr, os, orr, fs, fr, ys, yr, own_sem, label_sem, out_sem,
):
    local, nz, nx, ny = c_hbm.shape
    phases = h_ref.shape[0]
    me = lax.axis_index("comp")
    core = lax.rem(me, 2)
    spot = lax.rem(me // 2, inner)
    row = me // (2 * inner)

    def index(a, b, k):
        return (a * inner + b) * 2 + k

    sibling = index(row, spot, 1 - core)
    across = index(1 - row, spot, core)
    slot = spot * 2 + core
    peers = [index(row, lax.rem(spot + d, inner), core) for d in range(1, inner)]
    sources = [lax.rem(spot + inner - d, inner) * 2 + core for d in range(1, inner)]

    def remote(src, dst, send, recv, device):
        return pltpu.make_async_remote_copy(
            src_ref=src, dst_ref=dst, send_sem=send, recv_sem=recv,
            device_id={"comp": device}, device_id_type=MESH,
        )

    def x_copy(d, s):
        return remote(c_hbm.at[:, s], gathered.at[slot, :, s], xs.at[d, s], xr.at[d, s], peers[d])

    def o_copy(s):
        return remote(c_hbm.at[:, s], gathered.at[slot, :, s], os.at[s], orr.at[s], sibling)

    def f_copy(d, s):
        place = gathered.at[sources[d], :, s]
        return remote(place, place, fs.at[d, s], fr.at[d, s], sibling)

    def y_copy(s):
        return remote(part_out.at[:, s], part_in.at[:, s], ys.at[s], yr.at[s], across)

    def out_copy(s):
        return pltpu.make_async_copy(pot.at[:, s], pot_hbm.at[:, s], out_sem.at[s])

    own_copy = pltpu.make_async_copy(c_hbm, gathered.at[slot], own_sem)
    label_copy = pltpu.make_async_copy(ph_hbm, labels, label_sem)
    own_copy.start()
    label_copy.start()

    barrier = pltpu.get_barrier_semaphore()
    others = peers + [sibling, across]
    for other in others:
        pl.semaphore_signal(barrier, inc=1, device_id={"comp": other}, device_id_type=MESH)
    pl.semaphore_wait(barrier, len(others))

    def send(s):
        for d in range(inner - 1):
            x_copy(d, s).start()
        o_copy(s).start()

    for s in range(min(DEPTH, nz)):
        send(s)
    own_copy.wait()
    label_copy.wait()

    def partials(s):
        def block(i, carry):
            cols = pl.ds(pl.multiple_of(i * LANES, LANES), LANES)
            phase = labels[s, :, cols]
            masks = [phase == p for p in range(1, phases)]
            sums = {}
            for j in range(2 * inner):
                for l in range(local):
                    value = gathered[j, l, s, :, cols]
                    column = (row * 2 * inner + j) * local + l
                    for side, owner in enumerate((across, me)):
                        for o in range(local):
                            line = owner * local + o
                            factor = h_ref[0, line, column]
                            for p in range(1, phases):
                                factor = jnp.where(masks[p - 1], h_ref[p, line, column], factor)
                            term = factor * value
                            key = (side, o)
                            sums[key] = sums[key] + term if key in sums else term
            for o in range(local):
                part_out[o, s, :, cols] = sums[0, o]
                pot[o, s, :, cols] = sums[1, o]
            return carry

        lax.fori_loop(0, ny // LANES, block, 0)

    def finish(s):
        def block(i, carry):
            cols = pl.ds(pl.multiple_of(i * LANES, LANES), LANES)
            for o in range(local):
                own = gathered[slot, o, s, :, cols]
                pot[o, s, :, cols] = pot[o, s, :, cols] + part_in[o, s, :, cols] + own * own * own
            return carry

        lax.fori_loop(0, ny // LANES, block, 0)

    def step(t, carry):
        @pl.when(t < nz)
        def _():
            for d in range(inner - 1):
                x_copy(d, t).wait_recv()
                f_copy(d, t).start()

        @pl.when(t + DEPTH < nz)
        def _():
            send(t + DEPTH)

        @pl.when((t >= 1) & (t < nz + 1))
        def _():
            u = t - 1
            o_copy(u).wait_recv()
            for d in range(inner - 1):
                f_copy(d, u).wait_recv()
            partials(u)
            y_copy(u).start()

        @pl.when(t >= LAG)
        def _():
            v = t - LAG
            y_copy(v).wait_recv()
            finish(v)
            out_copy(v).start()

        return carry

    lax.fori_loop(0, nz + LAG, step, 0)

    def drain(s, carry):
        for d in range(inner - 1):
            x_copy(d, s).wait_send()
            f_copy(d, s).wait_send()
        o_copy(s).wait_send()
        y_copy(s).wait_send()
        out_copy(s).wait()
        return carry

    lax.fori_loop(0, nz, drain, 0)


def potentials(concentration, phase_labels, hessian):
    local, nz, nx, ny = concentration.shape
    inner = lax.axis_size("comp") // 4
    full = (local, nz, nx, ny)
    dma = pltpu.SemaphoreType.DMA
    return pl.pallas_call(
        functools.partial(potential_kernel, inner),
        out_shape=jax.ShapeDtypeStruct(full, jnp.float32),
        in_specs=[
            pl.BlockSpec(memory_space=pl.ANY),
            pl.BlockSpec(memory_space=pl.ANY),
            pl.BlockSpec(memory_space=pltpu.SMEM),
        ],
        out_specs=pl.BlockSpec(memory_space=pl.ANY),
        scratch_shapes=[
            pltpu.VMEM((2 * inner,) + full, jnp.float32),
            pltpu.VMEM((nz, nx, ny), jnp.int32),
            pltpu.VMEM(full, jnp.float32),
            pltpu.VMEM(full, jnp.float32),
            pltpu.VMEM(full, jnp.float32),
            dma((inner - 1, nz)), dma((inner - 1, nz)),
            dma((nz,)), dma((nz,)),
            dma((inner - 1, nz)), dma((inner - 1, nz)),
            dma((nz,)), dma((nz,)),
            dma, dma, dma((nz,)),
        ],
        compiler_params=pltpu.CompilerParams(
            collective_id=0, has_side_effects=True, vmem_limit_bytes=48 * 2**20
        ),
    )(concentration, phase_labels, hessian)


def on_device(concentration, phase_labels, hessian, mobility):
    local_comps = concentration.shape[0]
    comp_rank = lax.axis_index("comp")
    potential = potentials(concentration, phase_labels, hessian)
    own_mobility = lax.dynamic_slice_in_dim(mobility, comp_rank * local_comps, local_comps, 1)
    mobile = jnp.zeros(concentration.shape, jnp.float32)
    for phase in range(own_mobility.shape[0]):
        mobile = mobile + jnp.where(
            phase_labels == phase, own_mobility[phase][:, None, None, None], 0.0
        )
    padded = extended(potential, (("space", 2),), 1)
    source = concentration + time_step * mobile * laplace_inner(padded)
    bilap_coef = stiff_step * mobile
    diagonal_term = 1.0 + 42.0 * bilap_coef
    iterate = source
    for sweep in range(SWEEPS):
        widened = extended(iterate, (("space", 2),), 2)
        iterate = (
            iterate
            + damping
            * (source - iterate - bilap_coef * laplace_inner(laplace_inner(widened)))
            / diagonal_term
        )
    return (iterate, potential)


def solution(mesh):
    in_specs = (P("comp", None, "space", None), P(None, "space", None), P(), P())
    out_specs = (P("comp", None, "space", None), P("comp", None, "space", None))
    return jax.shard_map(
        on_device, mesh=mesh, in_specs=in_specs, out_specs=out_specs, check_vma=False
    )
```

```python
import functools

import jax
import jax.numpy as jnp
from jax import lax
from jax.experimental import pallas as pl
from jax.experimental.pallas import tpu as pltpu
from jax.sharding import PartitionSpec as P

time_step = 0.1
stiff_step = 0.02
damping = 0.5

MESH = pl.DeviceIdType.MESH
DEPTH = 3
LAG = 3
LANES = 256
EDGE = 4


def laplace(field, before, after, above, below):
    summed = before + after + above + below
    summed = summed + pltpu.roll(field, 1, 1) + pltpu.roll(field, field.shape[1] - 1, 1)
    return summed - 6.0 * field


def brick_kernel(
    inner, c_hbm, ph_hbm, h_ref, table, new_hbm, pot_hbm,
    gathered, labels, part_out, part_in, pot, source, twice, first,
    label_out, label_in, pot_out, pot_in, src_out, src_in,
    xs, xr, os, orr, fs, fr, ys, yr, own_sem, label_sem, out_sem, new_sem,
    ls, lr, ps, pr, ss, sr,
):
    local, nz, nx, ny = c_hbm.shape
    phases = h_ref.shape[0]
    me = lax.axis_index("comp")
    core = lax.rem(me, 2)
    spot = lax.rem(me // 2, inner)
    row = me // (2 * inner)

    def index(a, b, k):
        return (a * inner + b) * 2 + k

    sibling = index(row, spot, 1 - core)
    across = index(1 - row, spot, core)
    slot = spot * 2 + core
    peers = [index(row, lax.rem(spot + d, inner), core) for d in range(1, inner)]
    sources = [lax.rem(spot + inner - d, inner) * 2 + core for d in range(1, inner)]

    def remote(src, dst, send, recv, device):
        return pltpu.make_async_remote_copy(
            src_ref=src, dst_ref=dst, send_sem=send, recv_sem=recv,
            device_id={"comp": device}, device_id_type=MESH,
        )

    place_x = lax.axis_index("space")
    bricks = lax.axis_size("space")
    beside = (lax.rem(place_x + 1, bricks), lax.rem(place_x + bricks - 1, bricks))

    def aside(src, dst, send, recv, side):
        return pltpu.make_async_remote_copy(
            src_ref=src, dst_ref=dst, send_sem=send, recv_sem=recv,
            device_id={"space": beside[side]}, device_id_type=MESH,
        )

    def x_copy(d, s):
        return remote(c_hbm.at[:, s], gathered.at[slot, :, s], xs.at[d, s], xr.at[d, s], peers[d])

    def o_copy(s):
        return remote(c_hbm.at[:, s], gathered.at[slot, :, s], os.at[s], orr.at[s], sibling)

    def f_copy(d, s):
        place = gathered.at[sources[d], :, s]
        return remote(place, place, fs.at[d, s], fr.at[d, s], sibling)

    def y_copy(s):
        return remote(part_out.at[:, s], part_in.at[:, s], ys.at[s], yr.at[s], across)

    def l_copy(side):
        return aside(label_out.at[side], label_in.at[side], ls.at[side], lr.at[side], side)

    def p_copy(side, s):
        return aside(pot_out.at[side, :, s], pot_in.at[side, :, s], ps.at[side, s], pr.at[side, s], side)

    def s_copy(side, s):
        return aside(src_out.at[side, :, s], src_in.at[side, :, s], ss.at[side, s], sr.at[side, s], side)

    def new_copy(s):
        return pltpu.make_async_copy(part_in.at[:, s], new_hbm.at[:, s], new_sem.at[s])

    def out_copy(s):
        return pltpu.make_async_copy(pot.at[:, s], pot_hbm.at[:, s], out_sem.at[s])

    own_copy = pltpu.make_async_copy(c_hbm, gathered.at[slot], own_sem)
    label_copy = pltpu.make_async_copy(ph_hbm, labels.at[:, 0:nx], label_sem)
    own_copy.start()
    label_copy.start()

    barrier = pltpu.get_barrier_semaphore()
    others = peers + [sibling, across]
    for other in others:
        pl.semaphore_signal(barrier, inc=1, device_id={"comp": other}, device_id_type=MESH)
    for brick in beside:
        pl.semaphore_signal(barrier, inc=1, device_id={"space": brick}, device_id_type=MESH)
    pl.semaphore_wait(barrier, len(others) + 2)

    def send(s):
        for d in range(inner - 1):
            x_copy(d, s).start()
        o_copy(s).start()

    for s in range(min(DEPTH, nz)):
        send(s)
    own_copy.wait()
    label_copy.wait()

    def label_edges(z, carry):
        label_out[0, z] = labels[z, nx - EDGE : nx, :]
        label_out[1, z] = labels[z, 0:EDGE, :]
        return carry

    lax.fori_loop(0, nz, label_edges, 0)
    l_copy(0).start()
    l_copy(1).start()

    def partials(s):
        def block(i, carry):
            cols = pl.ds(pl.multiple_of(i * LANES, LANES), LANES)
            phase = labels[s, 0:nx, cols]
            masks = [phase == p for p in range(1, phases)]
            sums = {}
            for j in range(2 * inner):
                for l in range(local):
                    value = gathered[j, l, s, :, cols]
                    column = (row * 2 * inner + j) * local + l
                    for side, owner in enumerate((across, me)):
                        for o in range(local):
                            line = owner * local + o
                            factor = h_ref[0, line, column]
                            for p in range(1, phases):
                                factor = jnp.where(masks[p - 1], h_ref[p, line, column], factor)
                            term = factor * value
                            key = (side, o)
                            sums[key] = sums[key] + term if key in sums else term
            for o in range(local):
                part_out[o, s, :, cols] = sums[0, o]
                pot[o, s, :, cols] = sums[1, o]
            return carry

        lax.fori_loop(0, ny // LANES, block, 0)

    def finish(s):
        def block(i, carry):
            cols = pl.ds(pl.multiple_of(i * LANES, LANES), LANES)
            for o in range(local):
                own = gathered[slot, o, s, :, cols]
                pot[o, s, :, cols] = pot[o, s, :, cols] + part_in[o, s, :, cols] + own * own * own
            return carry

        lax.fori_loop(0, ny // LANES, block, 0)
        for o in range(local):
            pot_out[0, o, s] = pot[o, s, nx - 1 : nx, :]
            pot_out[1, o, s] = pot[o, s, 0:1, :]

    def plane(z):
        return lax.rem(z, nz)

    def chosen(kind, l, phase):
        result = table[kind, 0, me * local + l]
        for p in range(1, phases):
            result = jnp.where(phase == p, table[kind, p, me * local + l], result)
        return result

    def make_source(z):
        now, low, high = plane(z), plane(z + nz - 1), plane(z + 1)
        for side in range(2):
            p_copy(side, now).wait_recv()

        def component(l, carry):
            field = pot[l, now]
            line = lax.broadcasted_iota(jnp.int32, field.shape, 0)
            before = jnp.where(line == 0, pot_in[0, l, now], pltpu.roll(field, 1, 0))
            after = jnp.where(line == nx - 1, pot_in[1, l, now], pltpu.roll(field, nx - 1, 0))
            lap = laplace(field, before, after, pot[l, low], pot[l, high])
            value = gathered[slot, l, now] + chosen(0, l, labels[now, 0:nx, :]) * lap
            source[l, now, 0:nx, :] = value
            src_out[0, l, now] = value[nx - EDGE : nx]
            src_out[1, l, now] = value[0:EDGE]
            return carry

        lax.fori_loop(0, local, component, 0)
        for side in range(2):
            s_copy(side, now).start()

    def take_edges(z):
        now = plane(z)
        for side in range(2):
            s_copy(side, now).wait_recv()
        for l in range(local):
            source[l, now, nx : nx + EDGE, :] = src_in[1, l, now]
            source[l, now, nx + EDGE : nx + 2 * EDGE, :] = src_in[0, l, now]

    def once(ref, l, z, rows):
        now, low, high = plane(z), plane(z + nz - 1), plane(z + 1)
        field = ref[l, now]
        before = pltpu.roll(field, 1, 0)
        after = pltpu.roll(field, field.shape[0] - 1, 0)
        cut = slice(0, rows)
        return laplace(field[cut], before[cut], after[cut], ref[l, low, cut, :], ref[l, high, cut, :])

    wide = nx + 2 * EDGE

    def half(ref, z):
        def component(l, carry):
            twice[l, plane(z)] = once(ref, l, z, wide)
            return carry

        lax.fori_loop(0, local, component, 0)

    def sweep(ref, z, rows, store):
        now = plane(z)

        def component(l, carry):
            phase = labels[now, 0:rows, :]
            old = ref[l, now, 0:rows, :]
            bend = chosen(1, l, phase) * once(twice, l, z, rows)
            store[l, now] = old + chosen(2, l, phase) * (source[l, now, 0:rows, :] - old - bend)
            return carry

        lax.fori_loop(0, local, component, 0)

    def step(t, carry):
        @pl.when(t < nz)
        def _():
            for d in range(inner - 1):
                x_copy(d, t).wait_recv()
                f_copy(d, t).start()

        @pl.when(t + DEPTH < nz)
        def _():
            send(t + DEPTH)

        @pl.when((t >= 1) & (t < nz + 1))
        def _():
            u = t - 1
            o_copy(u).wait_recv()
            for d in range(inner - 1):
                f_copy(d, u).wait_recv()
            partials(u)
            y_copy(u).start()

        @pl.when((t >= LAG) & (t < nz + LAG))
        def _():
            v = t - LAG
            y_copy(v).wait_recv()
            finish(v)
            out_copy(v).start()
            for side in range(2):
                p_copy(side, v).start()

        @pl.when(t == LAG)
        def _():
            for side in range(2):
                l_copy(side).wait_recv()

            def widen(z, carry):
                labels[z, nx : nx + EDGE, :] = label_in[1, z]
                labels[z, nx + EDGE : nx + 2 * EDGE, :] = label_in[0, z]
                return carry

            lax.fori_loop(0, nz, widen, 0)

        w = t - LAG - 2

        @pl.when((w >= 1) & (w < nz + 1))
        def _():
            make_source(w)

        @pl.when((w - 2 >= 1) & (w - 2 < nz + 1))
        def _():
            take_edges(w - 2)

        @pl.when((w - 3 >= 2) & (w - 3 < nz + 2))
        def _():
            half(source, w - 3)

        @pl.when((w - 4 >= 3) & (w - 4 < nz + 3))
        def _():
            sweep(source, w - 4, wide, first)

        @pl.when((w - 5 >= 4) & (w - 5 < nz + 4))
        def _():
            half(first, w - 5)

        @pl.when(w - 6 >= 5)
        def _():
            sweep(first, w - 6, nx, part_in)
            new_copy(plane(w - 6)).start()

        return carry

    lax.fori_loop(0, nz + 5 + LAG + 8, step, 0)
    for side in range(2):
        l_copy(side).wait_send()

    def drain(s, carry):
        for d in range(inner - 1):
            x_copy(d, s).wait_send()
            f_copy(d, s).wait_send()
        o_copy(s).wait_send()
        y_copy(s).wait_send()
        out_copy(s).wait()
        new_copy(s).wait()
        for side in range(2):
            p_copy(side, s).wait_send()
            s_copy(side, s).wait_send()
        return carry

    lax.fori_loop(0, nz, drain, 0)


def on_device(concentration, phase_labels, hessian, mobility):
    local, nz, nx, ny = concentration.shape
    inner = lax.axis_size("comp") // 4
    full = (local, nz, nx, ny)
    wide = (local, nz, nx + 2 * EDGE, ny)
    coef = stiff_step * mobility
    table = jnp.stack([time_step * mobility, coef, damping / (1.0 + 42.0 * coef)])
    dma = pltpu.SemaphoreType.DMA
    f32 = jnp.float32
    return pl.pallas_call(
        functools.partial(brick_kernel, inner),
        out_shape=[jax.ShapeDtypeStruct(full, f32)] * 2,
        in_specs=[
            pl.BlockSpec(memory_space=pl.ANY),
            pl.BlockSpec(memory_space=pl.ANY),
            pl.BlockSpec(memory_space=pltpu.SMEM),
            pl.BlockSpec(memory_space=pltpu.SMEM),
        ],
        out_specs=[pl.BlockSpec(memory_space=pl.ANY)] * 2,
        scratch_shapes=[
            pltpu.VMEM((2 * inner,) + full, f32),
            pltpu.VMEM(wide[1:], jnp.int32),
            pltpu.VMEM(full, f32),
            pltpu.VMEM(full, f32),
            pltpu.VMEM(full, f32),
            pltpu.VMEM(wide, f32),
            pltpu.VMEM(wide, f32),
            pltpu.VMEM(wide, f32),
            pltpu.VMEM((2, nz, EDGE, ny), jnp.int32),
            pltpu.VMEM((2, nz, EDGE, ny), jnp.int32),
            pltpu.VMEM((2, local, nz, 1, ny), f32),
            pltpu.VMEM((2, local, nz, 1, ny), f32),
            pltpu.VMEM((2, local, nz, EDGE, ny), f32),
            pltpu.VMEM((2, local, nz, EDGE, ny), f32),
            dma((inner - 1, nz)), dma((inner - 1, nz)),
            dma((nz,)), dma((nz,)),
            dma((inner - 1, nz)), dma((inner - 1, nz)),
            dma((nz,)), dma((nz,)),
            dma, dma, dma((nz,)), dma((nz,)),
            dma((2,)), dma((2,)),
            dma((2, nz)), dma((2, nz)), dma((2, nz)), dma((2, nz)),
        ],
        compiler_params=pltpu.CompilerParams(
            collective_id=0, has_side_effects=True, vmem_limit_bytes=60 * 2**20
        ),
    )(concentration, phase_labels, hessian, table)


def solution(mesh):
    in_specs = (P("comp", None, "space", None), P(None, "space", None), P(), P())
    out_specs = (P("comp", None, "space", None), P("comp", None, "space", None))
    return jax.shard_map(
        on_device, mesh=mesh, in_specs=in_specs, out_specs=out_specs, check_vma=False
    )
```

```python
import functools

import jax
import jax.numpy as jnp
from jax import lax
from jax.experimental import pallas as pl
from jax.experimental.pallas import tpu as pltpu
from jax.sharding import PartitionSpec as P

time_step = 0.1
stiff_step = 0.02
damping = 0.5

MESH = pl.DeviceIdType.MESH
PARTS = 2
DEPTH = 7
LAG = 5
LANES = 256
EDGE = 4


def laplace(field, before, after, above, below):
    summed = before + after + above + below
    summed = summed + pltpu.roll(field, 1, 1) + pltpu.roll(field, field.shape[1] - 1, 1)
    return summed - 6.0 * field


def brick_kernel(
    inner, c_hbm, ph_hbm, h_ref, table, fresh, pot,
    gathered, labels, part_out, part_in, source, twice, first,
    label_out, label_in, pot_out, pot_in, src_out, src_in,
    xs, xr, os, orr, fs, fr, ys, yr, own_sem, label_sem,
    ls, lr, ps, pr, ss, sr,
):
    local, nz, nx, ny = c_hbm.shape
    phases = h_ref.shape[0]
    me = lax.axis_index("comp")
    core = lax.rem(me, 2)
    spot = lax.rem(me // 2, inner)
    row = me // (2 * inner)

    def index(a, b, k):
        return (a * inner + b) * 2 + k

    sibling = index(row, spot, 1 - core)
    across = index(1 - row, spot, core)
    slot = spot * 2 + core
    peers = [index(row, lax.rem(spot + d, inner), core) for d in range(1, inner)]
    sources = [lax.rem(spot + inner - d, inner) * 2 + core for d in range(1, inner)]

    def remote(src, dst, send, recv, device):
        return pltpu.make_async_remote_copy(
            src_ref=src, dst_ref=dst, send_sem=send, recv_sem=recv,
            device_id={"comp": device}, device_id_type=MESH,
        )

    place_x = lax.axis_index("space")
    bricks = lax.axis_size("space")
    beside = (lax.rem(place_x + 1, bricks), lax.rem(place_x + bricks - 1, bricks))

    def aside(src, dst, send, recv, side):
        return pltpu.make_async_remote_copy(
            src_ref=src, dst_ref=dst, send_sem=send, recv_sem=recv,
            device_id={"space": beside[side]}, device_id_type=MESH,
        )

    units = nz * PARTS
    span = ny // PARTS

    def unit(s):
        return s // PARTS, pl.ds(pl.multiple_of(lax.rem(s, PARTS) * span, 128), span)

    def x_copy(d, s):
        z, cols = unit(s)
        return remote(
            c_hbm.at[:, z, :, cols], gathered.at[slot, :, z, :, cols], xs.at[d, s], xr.at[d, s], peers[d]
        )

    def o_copy(s):
        z, cols = unit(s)
        return remote(c_hbm.at[:, z, :, cols], gathered.at[slot, :, z, :, cols], os.at[s], orr.at[s], sibling)

    def f_copy(d, s):
        z, cols = unit(s)
        place = gathered.at[sources[d], :, z, :, cols]
        return remote(place, place, fs.at[d, s], fr.at[d, s], sibling)

    def y_copy(s):
        z, cols = unit(s)
        return remote(part_out.at[:, z, :, cols], part_in.at[:, z, :, cols], ys.at[s], yr.at[s], across)

    def l_copy(side):
        return aside(label_out.at[side], label_in.at[side], ls.at[side], lr.at[side], side)

    def p_copy(side, s):
        return aside(pot_out.at[side, :, s], pot_in.at[side, :, s], ps.at[side, s], pr.at[side, s], side)

    def s_copy(side, s):
        return aside(src_out.at[side, :, s], src_in.at[side, :, s], ss.at[side, s], sr.at[side, s], side)

    own_copy = pltpu.make_async_copy(c_hbm, gathered.at[slot], own_sem)
    label_copy = pltpu.make_async_copy(ph_hbm, labels.at[:, 0:nx], label_sem)
    own_copy.start()
    label_copy.start()

    barrier = pltpu.get_barrier_semaphore()
    others = peers + [sibling, across]
    for other in others:
        pl.semaphore_signal(barrier, inc=1, device_id={"comp": other}, device_id_type=MESH)
    for brick in beside:
        pl.semaphore_signal(barrier, inc=1, device_id={"space": brick}, device_id_type=MESH)
    pl.semaphore_wait(barrier, len(others) + 2)

    def send(s):
        for d in range(inner - 1):
            x_copy(d, s).start()
        o_copy(s).start()

    for s in range(min(DEPTH, units)):
        send(s)
    own_copy.wait()
    label_copy.wait()

    def label_edges(z, carry):
        label_out[0, z] = labels[z, nx - EDGE : nx, :]
        label_out[1, z] = labels[z, 0:EDGE, :]
        return carry

    lax.fori_loop(0, nz, label_edges, 0)
    l_copy(0).start()
    l_copy(1).start()

    def partials(unit_index):
        s = unit_index // PARTS
        begin = lax.rem(unit_index, PARTS) * span

        def block(i, carry):
            cols = pl.ds(pl.multiple_of(begin + i * LANES, 128), LANES)
            phase = labels[s, 0:nx, cols]
            masks = [phase == p for p in range(1, phases)]
            sums = {}
            for j in range(2 * inner):
                for l in range(local):
                    value = gathered[j, l, s, :, cols]
                    column = (row * 2 * inner + j) * local + l
                    for side, owner in enumerate((across, me)):
                        for o in range(local):
                            line = owner * local + o
                            factor = h_ref[0, line, column]
                            for p in range(1, phases):
                                factor = jnp.where(masks[p - 1], h_ref[p, line, column], factor)
                            term = factor * value
                            key = (side, o)
                            sums[key] = sums[key] + term if key in sums else term
            for o in range(local):
                part_out[o, s, :, cols] = sums[0, o]
                pot[o, s, :, cols] = sums[1, o]
            return carry

        lax.fori_loop(0, span // LANES, block, 0)

    def finish(unit_index):
        s = unit_index // PARTS
        begin = lax.rem(unit_index, PARTS) * span

        def block(i, carry):
            cols = pl.ds(pl.multiple_of(begin + i * LANES, 128), LANES)
            for o in range(local):
                own = gathered[slot, o, s, :, cols]
                pot[o, s, :, cols] = pot[o, s, :, cols] + part_in[o, s, :, cols] + own * own * own
            return carry

        lax.fori_loop(0, span // LANES, block, 0)

    def edges(s):
        for o in range(local):
            pot_out[0, o, s] = pot[o, s, nx - 1 : nx, :]
            pot_out[1, o, s] = pot[o, s, 0:1, :]

    def plane(z):
        return lax.rem(z, nz)

    def chosen(kind, l, phase):
        result = table[kind, 0, me * local + l]
        for p in range(1, phases):
            result = jnp.where(phase == p, table[kind, p, me * local + l], result)
        return result

    def make_source(z):
        now, low, high = plane(z), plane(z + nz - 1), plane(z + 1)
        for side in range(2):
            p_copy(side, now).wait_recv()

        def component(l, carry):
            field = pot[l, now]
            line = lax.broadcasted_iota(jnp.int32, field.shape, 0)
            before = jnp.where(line == 0, pot_in[0, l, now], pltpu.roll(field, 1, 0))
            after = jnp.where(line == nx - 1, pot_in[1, l, now], pltpu.roll(field, nx - 1, 0))
            lap = laplace(field, before, after, pot[l, low], pot[l, high])
            value = gathered[slot, l, now] + chosen(0, l, labels[now, 0:nx, :]) * lap
            source[l, now, 0:nx, :] = value
            src_out[0, l, now] = value[nx - EDGE : nx]
            src_out[1, l, now] = value[0:EDGE]
            return carry

        lax.fori_loop(0, local, component, 0)
        for side in range(2):
            s_copy(side, now).start()

    def take_edges(z):
        now = plane(z)
        for side in range(2):
            s_copy(side, now).wait_recv()
        for l in range(local):
            source[l, now, nx : nx + EDGE, :] = src_in[1, l, now]
            source[l, now, nx + EDGE : nx + 2 * EDGE, :] = src_in[0, l, now]

    def once(ref, l, z, rows):
        now, low, high = plane(z), plane(z + nz - 1), plane(z + 1)
        field = ref[l, now]
        before = pltpu.roll(field, 1, 0)
        after = pltpu.roll(field, field.shape[0] - 1, 0)
        cut = slice(0, rows)
        return laplace(field[cut], before[cut], after[cut], ref[l, low, cut, :], ref[l, high, cut, :])

    wide = nx + 2 * EDGE

    def half(ref, z):
        def component(l, carry):
            twice[l, plane(z)] = once(ref, l, z, wide)
            return carry

        lax.fori_loop(0, local, component, 0)

    def sweep(ref, z, rows, store):
        now = plane(z)

        def component(l, carry):
            phase = labels[now, 0:rows, :]
            old = ref[l, now, 0:rows, :]
            bend = chosen(1, l, phase) * once(twice, l, z, rows)
            store[l, now] = old + chosen(2, l, phase) * (source[l, now, 0:rows, :] - old - bend)
            return carry

        lax.fori_loop(0, local, component, 0)

    def planes(z):
        @pl.when(z < nz)
        def _():
            edges(z)
            for side in range(2):
                p_copy(side, z).start()

        @pl.when(z == 0)
        def _():
            for side in range(2):
                l_copy(side).wait_recv()

            def widen(z, carry):
                labels[z, nx : nx + EDGE, :] = label_in[1, z]
                labels[z, nx + EDGE : nx + 2 * EDGE, :] = label_in[0, z]
                return carry

            lax.fori_loop(0, nz, widen, 0)

        w = z - 1

        @pl.when((w >= 1) & (w < nz + 1))
        def _():
            make_source(w)

        @pl.when((w - 2 >= 1) & (w - 2 < nz + 1))
        def _():
            take_edges(w - 2)

        @pl.when((w - 3 >= 2) & (w - 3 < nz + 2))
        def _():
            half(source, w - 3)

        @pl.when((w - 4 >= 3) & (w - 4 < nz + 3))
        def _():
            sweep(source, w - 4, wide, first)

        @pl.when((w - 5 >= 4) & (w - 5 < nz + 4))
        def _():
            half(first, w - 5)

        @pl.when(w - 6 >= 5)
        def _():
            sweep(first, w - 6, nx, fresh)

    def step(t, carry):
        @pl.when(t < units)
        def _():
            for d in range(inner - 1):
                x_copy(d, t).wait_recv()
                f_copy(d, t).start()

        @pl.when(t + DEPTH < units)
        def _():
            send(t + DEPTH)

        @pl.when((t >= 1) & (t < units + 1))
        def _():
            u = t - 1
            o_copy(u).wait_recv()
            for d in range(inner - 1):
                f_copy(d, u).wait_recv()
            partials(u)
            y_copy(u).start()

        v = t - LAG

        @pl.when((t >= LAG) & (t < units + LAG))
        def _():
            y_copy(v).wait_recv()
            finish(v)

        @pl.when((t >= LAG) & (lax.rem(t - LAG + PARTS, PARTS) == PARTS - 1))
        def _():
            planes(v // PARTS)

        return carry

    lax.fori_loop(0, LAG + units + 12 * PARTS, step, 0)
    for side in range(2):
        l_copy(side).wait_send()

    def drain_units(s, carry):
        for d in range(inner - 1):
            x_copy(d, s).wait_send()
            f_copy(d, s).wait_send()
        o_copy(s).wait_send()
        y_copy(s).wait_send()
        return carry

    lax.fori_loop(0, units, drain_units, 0)

    def drain(s, carry):
        for side in range(2):
            p_copy(side, s).wait_send()
            s_copy(side, s).wait_send()
        return carry

    lax.fori_loop(0, nz, drain, 0)


def on_device(concentration, phase_labels, hessian, mobility):
    local, nz, nx, ny = concentration.shape
    inner = lax.axis_size("comp") // 4
    full = (local, nz, nx, ny)
    wide = (local, nz, nx + 2 * EDGE, ny)
    coef = stiff_step * mobility
    table = jnp.stack([time_step * mobility, coef, damping / (1.0 + 42.0 * coef)])
    dma = pltpu.SemaphoreType.DMA
    f32 = jnp.float32
    return pl.pallas_call(
        functools.partial(brick_kernel, inner),
        out_shape=[pltpu.VMEM(full, f32)] * 2,
        in_specs=[
            pl.BlockSpec(memory_space=pl.ANY),
            pl.BlockSpec(memory_space=pl.ANY),
            pl.BlockSpec(memory_space=pltpu.SMEM),
            pl.BlockSpec(memory_space=pltpu.SMEM),
        ],
        out_specs=[pl.BlockSpec(memory_space=pltpu.VMEM)] * 2,
        scratch_shapes=[
            pltpu.VMEM((2 * inner,) + full, f32),
            pltpu.VMEM(wide[1:], jnp.int32),
            pltpu.VMEM(full, f32),
            pltpu.VMEM(full, f32),
            pltpu.VMEM(wide, f32),
            pltpu.VMEM(wide, f32),
            pltpu.VMEM(wide, f32),
            pltpu.VMEM((2, nz, EDGE, ny), jnp.int32),
            pltpu.VMEM((2, nz, EDGE, ny), jnp.int32),
            pltpu.VMEM((2, local, nz, 1, ny), f32),
            pltpu.VMEM((2, local, nz, 1, ny), f32),
            pltpu.VMEM((2, local, nz, EDGE, ny), f32),
            pltpu.VMEM((2, local, nz, EDGE, ny), f32),
            dma((inner - 1, nz * PARTS)), dma((inner - 1, nz * PARTS)),
            dma((nz * PARTS,)), dma((nz * PARTS,)),
            dma((inner - 1, nz * PARTS)), dma((inner - 1, nz * PARTS)),
            dma((nz * PARTS,)), dma((nz * PARTS,)),
            dma, dma,
            dma((2,)), dma((2,)),
            dma((2, nz)), dma((2, nz)), dma((2, nz)), dma((2, nz)),
        ],
        compiler_params=pltpu.CompilerParams(
            collective_id=0, has_side_effects=True, vmem_limit_bytes=54 * 2**20
        ),
    )(concentration, phase_labels, hessian, table)


def solution(mesh):
    in_specs = (P("comp", None, "space", None), P(None, "space", None), P(), P())
    out_specs = (P("comp", None, "space", None), P("comp", None, "space", None))
    return jax.shard_map(
        on_device, mesh=mesh, in_specs=in_specs, out_specs=out_specs, check_vma=False
    )
```
